32 devices in a mesh: groups: 2 (over y), expert: 4 (over z), dp: 2 (over x), sub: 2 (over core).
Axes of the slice: x: 2, y: 2, z: 4, core: 2. Of those that a mesh axis runs over, the one named last changes fastest.
Arguments:
- tokens: bfloat16 [4096, 1536], P(('groups', 'expert', 'dp', 'sub')), parts along dimension 0, may hold values from -6 to 6
- expert_ids: int32 [4096, 2], P(('groups', 'expert', 'dp', 'sub')), parts along dimension 0, may hold values from 0 to 7, all different within a row; in each aligned block of 128 rows (0 to 127, 128 to 255, ...) at most 48 rows name the same one
- route_weights: bfloat16 [4096, 2], P(('groups', 'expert', 'dp', 'sub')), parts along dimension 0, may hold values from 0.125 to 1
- out_grad: bfloat16 [4096, 1536], P(('groups', 'expert', 'dp', 'sub')), parts along dimension 0, may hold values from -6 to 6
- gate_weight: bfloat16 [8, 384, 1536], P(('expert', 'dp'), 'sub'), may hold values from -0.15625 to 0.15625
- up_weight: bfloat16 [8, 384, 1536], P(('expert', 'dp'), 'sub'), may hold values from -0.15625 to 0.15625
- down_weight: bfloat16 [8, 384, 1536], P(('expert', 'dp'), 'sub'), may hold values from -0.3125 to 0.3125
Outputs:
- mixed: bfloat16 [4096, 1536], P(('groups', 'expert', 'dp', 'sub')), parts along dimension 0
- token_grad: bfloat16 [4096, 1536], P(('groups', 'expert', 'dp', 'sub')), parts along dimension 0
- route_grad: float32 [4096, 2], P(('groups', 'expert', 'dp', 'sub')), parts along dimension 0
- gate_grad: bfloat16 [16, 384, 1536], P(('groups', 'expert', 'dp'), 'sub'), parts along dimension 0
- up_grad: bfloat16 [16, 384, 1536], P(('groups', 'expert', 'dp'), 'sub'), parts along dimension 0
- down_grad: bfloat16 [16, 384, 1536], P(('groups', 'expert', 'dp'), 'sub'), parts along dimension 0
The draws below stay inside these ranges and needn't reach their ends.
There are 2 independent parts, one for each index of `groups`. The reference program is written for one: setup_inputs(seed, part) draws one part's arguments, and reference() takes and returns one part's arrays. A program takes and returns all parts, laid end to end along the dimension named above; an argument that names none is the same for every part. Nothing has to cross between parts.
Inputs may be any that keep to these rules, and one draw needn't show every extreme that they name: `expert_ids`: each row names 2 different experts. In the rows of one device (aligned blocks of 128 rows) no expert is named by more than 48 rows, a bound that some block reaches.
All inputs are finite; a program needn't handle non-finite values.
Results may differ from the reference program's by a relative error of at most 0.009.
Values may be sent and summed in bfloat16 or wider, within the bound.
A program may use at most 64 MiB of HBM per device.

```python
import math
import jax
import jax.numpy as jnp
import numpy as np
from jax import lax

D = 1536
FF = 384
TOP = 2
TOK_DEV = 128
EXPERTS = 8
CAP = 48
TOKENS = 2048
N_SUB = 2


def levels(rng, shape, shards, smallest, high):
    factor_of = 1.0
    for dim, shards_of in shards:
        heights = jax.random.uniform(jax.random.fold_in(jax.random.fold_in(rng, 6), dim), (shards_of,), jnp.float32, smallest / len(shards), high / len(shards))
        factor_of = factor_of * jnp.repeat(jnp.exp(heights), shape[dim] // shards_of).reshape((-1,) + (1,) * (len(shape) - 1 - dim))
    return factor_of


def shared_out(own_key, own, number, rows, count, top, bound, slope):
    ranking = jax.random.permutation(own_key, count)
    crowded, usual = shares(count, rows * top, bound, slope, True), shares(count, rows * top, bound, slope, False)
    places = jnp.arange(count)

    def named(sizes, offset_by):
        used = int((sizes > 0).sum())
        fixed = max(1, used // 4)
        moved = fixed + (places - fixed + offset_by * (used - fixed)) % max(1, count - fixed)
        return jnp.zeros((count,), jnp.int32).at[ranking[jnp.where(places < fixed, places, moved)]].set(jnp.asarray(sizes, jnp.int32))

    sizes = jnp.where(number % 4 == 0, named(crowded, number // 4), named(usual, number - number // 4 - 1))
    mixed = jax.random.permutation(jax.random.fold_in(own, 3), count)
    donor, receiver = mixed[0:count // 2 * 2:2], mixed[1:count // 2 * 2:2]
    slack = jnp.minimum(sizes[donor] - 1, bound - sizes[receiver]) // 2
    slack = jnp.where((donor == ranking[0]) | (receiver == ranking[0]) | (sizes[receiver] == 0), 0, jnp.maximum(slack, 0))
    moved = jax.random.randint(jax.random.fold_in(own, 4), (count // 2,), 0, 1 << 20) % (slack + 1)
    sizes = sizes.at[donor].add(-moved).at[receiver].add(moved)
    items = jnp.searchsorted(jnp.cumsum(sizes), jnp.arange(rows * top), side="right").astype(jnp.int32)
    grid = items.reshape(top, rows).T
    grid = grid[jax.random.permutation(jax.random.fold_in(own, 1), rows)]
    offset_by = jax.random.randint(jax.random.fold_in(own, 2), (rows, 1), 0, top)
    return jnp.take_along_axis(grid, (jnp.arange(top)[None, :] + offset_by) % top, axis=1)


def shares(amount, total, limit, lean, full):
    loads = [(1 << 20) // math.isqrt(rank ** lean) + 1 for rank in range(1, amount + 1)]
    largest = limit if full else min(limit, max(-(-total // amount), total * loads[0] // sum(loads)))
    least = 1 if total - largest >= amount - 1 else 0
    given, surplus = [largest] + [least] * (amount - 1), total - largest - least * (amount - 1)
    while surplus > 0:
        free = [i for i in range(1, amount) if given[i] < largest] or [i for i in range(1, amount) if given[i] < limit]
        pool, budget = sum([loads[i] for i in free]), surplus
        for i in free:
            extra = min(limit - given[i], max(1, budget * loads[i] // pool), surplus)
            given[i] = given[i] + extra
            surplus = surplus - extra
    return np.array(given)


def gaussian(stream_key, dims, width, bound, split=(), kind=jnp.bfloat16):
    array = jax.random.normal(stream_key, dims, jnp.float32) * width
    if len(split) > 0:
        array = levels(stream_key, dims, split, -0.22, 0.18) * array
    return jnp.clip(array, min=-bound, max=bound).astype(kind)


def setup_inputs(seed: int = 0, part: int = 0) -> dict:
    key_list = jax.random.split(jax.random.key(seed), 8)
    part_keys = jax.random.split(jax.random.fold_in(key_list[7], part), 8)
    tokens = gaussian(part_keys[0], (TOKENS, D), 1.0, 6.0, ((0, 16),))
    expert_ids_keys = jax.random.split(jax.random.fold_in(part_keys[1], 1), TOKENS // TOK_DEV)
    expert_ids_turns = jax.random.permutation(jax.random.fold_in(part_keys[1], 3), TOKENS // TOK_DEV)
    expert_ids = jax.vmap(lambda own, number: shared_out(jax.random.fold_in(part_keys[1], 2), own, number, TOK_DEV, EXPERTS, TOP, CAP, 2))(expert_ids_keys, expert_ids_turns).reshape((TOKENS, TOP))
    route_weights = jnp.clip(jnp.exp(math.log(1.0) - 2.0794415 * jax.random.uniform(part_keys[2], (TOKENS, TOP), jnp.float32) ** levels(part_keys[2], (TOKENS, TOP), ((0, 16),), -0.2, 0.2)), 0.125, 1.0).astype(jnp.bfloat16)
    out_grad = gaussian(part_keys[3], (TOKENS, D), 1.0, 6.0, ((0, 16),))
    gate_weight = gaussian(key_list[4], (EXPERTS, FF, D), D ** -0.5, 0.15625, ((0, 8), (1, 2)))
    up_weight = gaussian(key_list[5], (EXPERTS, FF, D), D ** -0.5, 0.15625, ((0, 8), (1, 2)))
    down_weight = gaussian(key_list[6], (EXPERTS, FF, D), FF ** -0.5, 0.3125, ((0, 8), (1, 2)))
    return {"tokens": tokens, "expert_ids": expert_ids, "route_weights": route_weights, "out_grad": out_grad, "gate_weight": gate_weight, "up_weight": up_weight, "down_weight": down_weight}


def reference(tokens, expert_ids, route_weights, out_grad, gate_weight, up_weight, down_weight):
    assigned = TOKENS * TOP
    blocks = TOKENS // TOK_DEV
    per_block = TOK_DEV * TOP
    block_ids = expert_ids.reshape(blocks, per_block)
    onehot = (block_ids[:, :, None] == jnp.arange(EXPERTS, dtype=jnp.int32)[None, None, :]).astype(jnp.int32)
    before = jnp.cumsum(onehot, axis=1) - onehot
    slot_index = jnp.sum(before * onehot, axis=2).reshape(-1).astype(jnp.int32)
    block_of = (jnp.arange(assigned, dtype=jnp.int32) // per_block).astype(jnp.int32)
    position = block_of * CAP + slot_index
    flat_ids = expert_ids.reshape(-1).astype(jnp.int32)
    table = jnp.full((EXPERTS, blocks * CAP), assigned, jnp.int32)
    table = table.at[flat_ids, position].set(jnp.arange(assigned, dtype=jnp.int32))
    zero_row = jnp.zeros((1, D), jnp.bfloat16)
    tokens_pad = jnp.concatenate([tokens, zero_row], axis=0)
    grad_pad = jnp.concatenate([out_grad, zero_row], axis=0)
    weight_pad = jnp.concatenate([route_weights.reshape(-1), jnp.zeros((1,), jnp.bfloat16)], axis=0)

    def one_expert(carry, inputs):
        mixed_acc, input_acc, route_acc = carry
        rows, gate_mat, up_mat, down_mat = inputs
        owner = (rows // TOP).astype(jnp.int32)
        rows_x = tokens_pad[owner]
        rows_dy = grad_pad[owner]
        visit_w = weight_pad[rows].astype(jnp.float32)
        gate = jnp.dot(rows_x, gate_mat.T, preferred_element_type=jnp.float32)
        up = jnp.dot(rows_x, up_mat.T, preferred_element_type=jnp.float32)
        sig = jax.nn.sigmoid(gate)
        hidden = (gate * sig * up).astype(jnp.bfloat16)
        expert_out = jnp.dot(hidden, down_mat, preferred_element_type=jnp.float32).astype(jnp.bfloat16)
        out_scaled = (visit_w[:, None] * rows_dy.astype(jnp.float32)).astype(jnp.bfloat16)
        hidden_grad = jnp.dot(out_scaled, down_mat.T, preferred_element_type=jnp.float32)
        gate_delta = (hidden_grad * up * sig * (1.0 + gate * (1.0 - sig))).astype(jnp.bfloat16)
        up_delta = (hidden_grad * gate * sig).astype(jnp.bfloat16)
        visit_grad = (jnp.dot(gate_delta, gate_mat, preferred_element_type=jnp.float32)
                      + jnp.dot(up_delta, up_mat, preferred_element_type=jnp.float32)).astype(jnp.bfloat16)
        mixed_acc = mixed_acc.at[owner].add(visit_w[:, None] * expert_out.astype(jnp.float32))
        input_acc = input_acc.at[owner].add(visit_grad.astype(jnp.float32))
        route_part = jnp.sum(rows_dy.astype(jnp.float32) * expert_out.astype(jnp.float32), axis=1)
        route_acc = route_acc.at[rows].set(route_part)
        pairs = blocks // N_SUB
        x_four = rows_x.astype(jnp.float32).reshape(pairs, N_SUB, CAP, D)
        dy_four = out_scaled.astype(jnp.float32).reshape(pairs, N_SUB, CAP, D)

        def class_sum(left, right):
            left_four = left.astype(jnp.float32).reshape(pairs, N_SUB, CAP, FF)
            partial_value = jnp.einsum("qscf,qscd->sfd", left_four, right).astype(jnp.bfloat16)
            return jnp.sum(partial_value.astype(jnp.float32), axis=0).astype(jnp.bfloat16)

        grads = (class_sum(gate_delta, x_four), class_sum(up_delta, x_four), class_sum(hidden, dy_four))
        return (mixed_acc, input_acc, route_acc), grads

    start = (jnp.zeros((TOKENS + 1, D), jnp.float32), jnp.zeros((TOKENS + 1, D), jnp.float32),
             jnp.zeros((assigned + 1,), jnp.float32))
    final, grads = lax.scan(one_expert, start, (table, gate_weight, up_weight, down_weight))
    mixed = final[0][:TOKENS].astype(jnp.bfloat16)
    token_grad = final[1][:TOKENS].astype(jnp.bfloat16)
    route_grad = final[2][:assigned].reshape(TOKENS, TOP)
    return (mixed, token_grad, route_grad, grads[0], grads[1], grads[2])
```

```python
import jax
import jax.numpy as jnp
from jax import lax
from jax.sharding import PartitionSpec as P


def expert_piece(rows_x, rows_grad, gate_piece, up_piece, down_piece):
    gate = jnp.einsum("rd,fd->rf", rows_x, gate_piece, preferred_element_type=jnp.float32)
    up_value = jnp.einsum("rd,fd->rf", rows_x, up_piece, preferred_element_type=jnp.float32)
    sigmoid = jax.nn.sigmoid(gate)
    hidden = (gate * sigmoid * up_value).astype(jnp.bfloat16)
    output = jnp.einsum("rf,fd->rd", hidden, down_piece, preferred_element_type=jnp.float32)
    hidden_grad = jnp.einsum("rd,fd->rf", rows_grad, down_piece, preferred_element_type=jnp.float32)
    gate_delta = (hidden_grad * up_value * sigmoid * (1.0 + gate * (1.0 - sigmoid))).astype(
        jnp.bfloat16
    )
    up_delta = (hidden_grad * gate * sigmoid).astype(jnp.bfloat16)
    input_grad = jnp.einsum(
        "rf,fd->rd", gate_delta, gate_piece, preferred_element_type=jnp.float32
    ) + jnp.einsum("rf,fd->rd", up_delta, up_piece, preferred_element_type=jnp.float32)
    gate_part = jnp.einsum("rf,rd->fd", gate_delta, rows_x, preferred_element_type=jnp.float32)
    up_part = jnp.einsum("rf,rd->fd", up_delta, rows_x, preferred_element_type=jnp.float32)
    down_part = jnp.einsum("rf,rd->fd", hidden, rows_grad, preferred_element_type=jnp.float32)
    return (output, input_grad, gate_part, up_part, down_part)


def shards(tokens, expert_ids, route_weights, out_grad, gate_weight, up_weight, down_weight):
    tok_rows, features = tokens.shape
    top_count = expert_ids.shape[1]
    expert_count = lax.axis_size("expert")
    replica_count = lax.axis_size("dp")
    experts = expert_count * replica_count
    capacity = max(2, 3 * tok_rows * top_count // (2 * experts))
    flat_ids = expert_ids.reshape(-1)
    onehot = (flat_ids[:, None] == jnp.arange(experts, dtype=jnp.int32)[None, :]).astype(jnp.int32)
    before = jnp.cumsum(onehot, axis=0) - onehot
    slot_index = jnp.sum(before * onehot, axis=1)
    target = flat_ids * capacity + slot_index
    rows_total = experts * capacity
    send_x = (
        jnp.zeros((rows_total, features), jnp.bfloat16)
        .at[target]
        .set(jnp.repeat(tokens, top_count, axis=0))
    )
    send_dy = (
        jnp.zeros((rows_total, features), jnp.bfloat16)
        .at[target]
        .set(jnp.repeat(out_grad, top_count, axis=0))
    )
    send_w = jnp.zeros((rows_total,), jnp.bfloat16).at[target].set(route_weights.reshape(-1))
    moved = (
        lax.all_to_all(
            send_x.reshape(experts, capacity, features),
            ("expert", "dp"),
            split_axis=0,
            concat_axis=0,
            tiled=True,
        ),
        lax.all_to_all(
            send_dy.reshape(experts, capacity, features),
            ("expert", "dp"),
            split_axis=0,
            concat_axis=0,
            tiled=True,
        ),
        lax.all_to_all(
            send_w.reshape(experts, capacity),
            ("expert", "dp"),
            split_axis=0,
            concat_axis=0,
            tiled=True,
        ),
    )
    recv_x = moved[0].reshape(rows_total, features)
    recv_dy = moved[1].reshape(rows_total, features)
    recv_w = moved[2].reshape(rows_total)
    scaled_grad = (recv_w[:, None].astype(jnp.float32) * recv_dy.astype(jnp.float32)).astype(
        jnp.bfloat16
    )
    out_part, grad_part, gate_part, up_part, down_part = expert_piece(
        recv_x,
        scaled_grad,
        lax.all_gather(gate_weight, "sub", axis=1, tiled=True)[0],
        lax.all_gather(up_weight, "sub", axis=1, tiled=True)[0],
        lax.all_gather(down_weight, "sub", axis=1, tiled=True)[0],
    )
    outputs = out_part.astype(jnp.bfloat16)
    input_grads = grad_part.astype(jnp.bfloat16)
    summed = (
        lax.psum_scatter(
            gate_part.astype(jnp.bfloat16), "sub", scatter_dimension=0, tiled=True
        ).astype(jnp.float32),
        lax.psum_scatter(
            up_part.astype(jnp.bfloat16), "sub", scatter_dimension=0, tiled=True
        ).astype(jnp.float32),
        lax.psum_scatter(
            down_part.astype(jnp.bfloat16), "sub", scatter_dimension=0, tiled=True
        ).astype(jnp.float32),
    )
    gate_grad = summed[0].astype(jnp.bfloat16)[None]
    up_grad = summed[1].astype(jnp.bfloat16)[None]
    down_grad = summed[2].astype(jnp.bfloat16)[None]
    returned = (
        lax.all_to_all(
            outputs.reshape(experts, capacity, features),
            ("expert", "dp"),
            split_axis=0,
            concat_axis=0,
            tiled=True,
        ),
        lax.all_to_all(
            input_grads.reshape(experts, capacity, features),
            ("expert", "dp"),
            split_axis=0,
            concat_axis=0,
            tiled=True,
        ),
    )
    back_out = returned[0].reshape(rows_total, features)[target]
    back_grad = returned[1].reshape(rows_total, features)[target]
    weights_flat = route_weights.reshape(-1).astype(jnp.float32)
    mixed = jnp.sum(
        (weights_flat[:, None] * back_out.astype(jnp.float32)).reshape(
            tok_rows, top_count, features
        ),
        axis=1,
    ).astype(jnp.bfloat16)
    token_grad = jnp.sum(
        back_grad.astype(jnp.float32).reshape(tok_rows, top_count, features), axis=1
    ).astype(jnp.bfloat16)
    route_grad = jnp.sum(
        jnp.repeat(out_grad, top_count, axis=0).astype(jnp.float32) * back_out.astype(jnp.float32),
        axis=1,
    ).reshape(tok_rows, top_count)
    return (mixed, token_grad, route_grad, gate_grad, up_grad, down_grad)


def shards_dense(tokens, expert_ids, route_weights, out_grad, gate_weight, up_weight, down_weight):
    rows, features = tokens.shape
    dp = lax.axis_size("dp")
    stages = lax.axis_size("expert")
    experts = stages * dp
    half = gate_weight.shape[1]
    f32, bf16 = jnp.float32, jnp.bfloat16
    which = jnp.arange(experts, dtype=jnp.int32)
    hit = expert_ids[:, :, None] == which[None, None, :]
    by_expert = jnp.sum(jnp.where(hit, route_weights.astype(f32)[:, :, None], 0.0), axis=1).astype(bf16)
    w_all = lax.all_gather(by_expert, "expert", axis=0, tiled=True)
    x_all = lax.all_gather(tokens, "expert", axis=0, tiled=True)
    gate_w = lax.all_gather(gate_weight[0], ("dp", "sub"), axis=0, tiled=True)
    up_w = lax.all_gather(up_weight[0], ("dp", "sub"), axis=0, tiled=True)
    down_w = lax.all_gather(down_weight[0], ("dp", "sub"), axis=0, tiled=True)
    dy_all = lax.all_gather(out_grad, "expert", axis=0, tiled=True)
    units = gate_w.shape[0]
    mine = lax.dynamic_slice_in_dim(w_all, lax.axis_index("expert") * dp, dp, axis=1).astype(f32)
    w_units = jnp.repeat(mine, units // dp, axis=1)
    gate = jnp.einsum("rd,fd->rf", x_all, gate_w, preferred_element_type=f32)
    up = jnp.einsum("rd,fd->rf", x_all, up_w, preferred_element_type=f32)
    sig = jax.nn.sigmoid(gate)
    hidden = gate * sig * up
    scaled = (w_units * hidden).astype(bf16)
    mixed_part = jnp.einsum("rf,fd->rd", scaled, down_w, preferred_element_type=f32).astype(bf16)
    mixed = lax.psum_scatter(mixed_part, "expert", scatter_dimension=0, tiled=True)
    back = jnp.einsum("rd,fd->rf", dy_all, down_w, preferred_element_type=f32)
    route = jnp.sum((hidden * back).reshape(stages, rows, dp, units // dp), axis=3)
    hidden_grad = w_units * back
    gate_delta = (hidden_grad * up * sig * (1.0 + gate * (1.0 - sig))).astype(bf16)
    up_delta = (hidden_grad * gate * sig).astype(bf16)
    token_part = (
        jnp.einsum("rf,fd->rd", gate_delta, gate_w, preferred_element_type=f32)
        + jnp.einsum("rf,fd->rd", up_delta, up_w, preferred_element_type=f32)
    ).astype(bf16)
    token_grad = lax.psum_scatter(token_part, "expert", scatter_dimension=0, tiled=True)

    def weight_grad(left, right):
        part = jnp.einsum("rf,rd->fd", left, right, preferred_element_type=f32).astype(bf16)
        return lax.psum_scatter(part, ("dp", "sub"), scatter_dimension=0, tiled=True)[None]

    down_grad = weight_grad(scaled, dy_all)
    gate_grad = weight_grad(gate_delta, x_all)
    up_grad = weight_grad(up_delta, x_all)
    routes = lax.all_to_all(route, "expert", split_axis=0, concat_axis=0, tiled=True)
    per_expert = routes.transpose(1, 0, 2).reshape(rows, experts)
    route_grad = jnp.sum(jnp.where(hit, per_expert[:, None, :], 0.0), axis=2)
    return (mixed, token_grad, route_grad, gate_grad, up_grad, down_grad)


def solution(mesh):
    placed = (
        P(("groups", "expert", "dp", "sub"), None),
        P(("groups", "expert", "dp", "sub"), None),
        P(("groups", "expert", "dp", "sub"), None),
        P(("groups", "expert", "dp", "sub"), None),
        P(("expert", "dp"), "sub", None),
        P(("expert", "dp"), "sub", None),
        P(("expert", "dp"), "sub", None),
    )
    body = shards_dense if mesh.shape["dp"] <= 2 else shards
    return jax.shard_map(
        body,
        mesh=mesh,
        in_specs=placed,
        out_specs=(
            P(("groups", "expert", "dp", "sub"), None),
            P(("groups", "expert", "dp", "sub"), None),
            P(("groups", "expert", "dp", "sub"), None),
            P(("groups", "expert", "dp"), "sub", None),
            P(("groups", "expert", "dp"), "sub", None),
            P(("groups", "expert", "dp"), "sub", None),
        ),
        check_vma=False,
    )
```

```python
import jax
import jax.numpy as jnp
from jax import lax
from jax.sharding import PartitionSpec as P


def shards(tokens, expert_ids, route_weights, out_grad, gate_weight, up_weight, down_weight):
    f32, bf16 = jnp.float32, jnp.bfloat16
    tok_rows, features = tokens.shape
    top_count = expert_ids.shape[1]
    experts = lax.axis_size("expert") * lax.axis_size("dp")
    capacity = max(2, 3 * tok_rows * top_count // (2 * experts))
    rows_total = experts * capacity

    hit = expert_ids[:, :, None] == jnp.arange(experts, dtype=jnp.int32)[None, None, :]
    named = jnp.any(hit, axis=1).astype(bf16)
    row = jnp.arange(tok_rows)
    earlier = (row[:, None] > row[None, :]).astype(bf16)
    before = jnp.dot(earlier, named, preferred_element_type=f32)
    slot_index = jnp.sum(jnp.where(hit, before[:, None, :], 0.0), axis=2).astype(jnp.int32)
    target = expert_ids * capacity + slot_index
    slots = jnp.arange(rows_total, dtype=jnp.int32)
    picks = target.T[:, :, None] == slots[None, None, :]
    pick = picks.astype(bf16)
    place = jnp.any(picks, axis=0).astype(bf16)
    weigh = jnp.sum(
        jnp.where(picks, route_weights.T.astype(f32)[:, :, None], 0.0), axis=0
    ).astype(bf16)

    def exchange(rows):
        moved = lax.all_to_all(
            rows.reshape(experts, capacity, features),
            ("expert", "dp"),
            split_axis=0,
            concat_axis=0,
            tiled=True,
        )
        return moved.reshape(rows_total, features)

    send_x = jnp.einsum("ts,td->sd", place, tokens, preferred_element_type=f32).astype(bf16)
    recv_x = exchange(send_x)
    send_dy = jnp.einsum("ts,td->sd", weigh, out_grad, preferred_element_type=f32).astype(bf16)
    recv_dy = exchange(send_dy)
    gate_full = lax.all_gather(gate_weight[0], "sub", axis=0, tiled=True)
    up_full = lax.all_gather(up_weight[0], "sub", axis=0, tiled=True)
    down_full = lax.all_gather(down_weight[0], "sub", axis=0, tiled=True)

    gate = jnp.einsum("rd,fd->rf", recv_x, gate_full, preferred_element_type=f32)
    up = jnp.einsum("rd,fd->rf", recv_x, up_full, preferred_element_type=f32)
    sigmoid = jax.nn.sigmoid(gate)
    hidden = (gate * sigmoid * up).astype(bf16)
    output = jnp.einsum("rf,fd->rd", hidden, down_full, preferred_element_type=f32).astype(bf16)
    back_out = exchange(output)

    hidden_grad = jnp.einsum("rd,fd->rf", recv_dy, down_full, preferred_element_type=f32)
    gate_delta = (hidden_grad * up * sigmoid * (1.0 + gate * (1.0 - sigmoid))).astype(bf16)
    up_delta = (hidden_grad * gate * sigmoid).astype(bf16)
    input_grad = (
        jnp.einsum("rf,fd->rd", gate_delta, gate_full, preferred_element_type=f32)
        + jnp.einsum("rf,fd->rd", up_delta, up_full, preferred_element_type=f32)
    ).astype(bf16)
    back_grad = exchange(input_grad)

    def weight_grad(left, right):
        part = jnp.einsum("rf,rd->fd", left, right, preferred_element_type=f32).astype(bf16)
        return lax.psum_scatter(part, "sub", scatter_dimension=0, tiled=True)[None]

    down_grad = weight_grad(hidden, recv_dy)
    gate_grad = weight_grad(gate_delta, recv_x)
    up_grad = weight_grad(up_delta, recv_x)

    weights = route_weights.astype(f32)
    cotangent = out_grad.astype(f32)
    visit = [jnp.dot(pick[k], back_out, preferred_element_type=f32) for k in range(top_count)]
    mixed = sum(weights[:, k : k + 1] * visit[k] for k in range(top_count)).astype(bf16)
    route_grad = jnp.stack([jnp.sum(cotangent * v, axis=1) for v in visit], axis=1)
    token_grad = jnp.einsum("ts,sd->td", place, back_grad, preferred_element_type=f32).astype(bf16)
    return (mixed, token_grad, route_grad, gate_grad, up_grad, down_grad)


def solution(mesh):
    rows = P(("groups", "expert", "dp", "sub"), None)
    weight = P(("expert", "dp"), "sub", None)
    grad = P(("groups", "expert", "dp"), "sub", None)
    return jax.shard_map(
        shards,
        mesh=mesh,
        in_specs=(rows,) * 4 + (weight,) * 3,
        out_specs=(rows,) * 3 + (grad,) * 3,
        check_vma=False,
    )
```

```python
import jax
import jax.numpy as jnp
from jax import lax
from jax.sharding import PartitionSpec as P


def shards(tokens, expert_ids, route_weights, out_grad, gate_weight, up_weight, down_weight):
    f32, bf16 = jnp.float32, jnp.bfloat16
    tok_rows, features = tokens.shape
    top_count = expert_ids.shape[1]
    experts = lax.axis_size("expert") * lax.axis_size("dp")
    capacity = max(2, 3 * tok_rows * top_count // (2 * experts))
    rows_total = experts * capacity

    hit = expert_ids[:, :, None] == jnp.arange(experts, dtype=jnp.int32)[None, None, :]
    named = jnp.any(hit, axis=1).astype(bf16)
    row = jnp.arange(tok_rows)
    earlier = (row[:, None] > row[None, :]).astype(bf16)
    before = jnp.dot(earlier, named, preferred_element_type=f32)
    slot_index = jnp.sum(jnp.where(hit, before[:, None, :], 0.0), axis=2).astype(jnp.int32)
    target = expert_ids * capacity + slot_index
    slots = jnp.arange(rows_total, dtype=jnp.int32)
    picks = target.T[:, :, None] == slots[None, None, :]
    pick = picks.astype(bf16)
    place = jnp.any(picks, axis=0).astype(bf16)
    weigh = jnp.sum(
        jnp.where(picks, route_weights.T.astype(f32)[:, :, None], 0.0), axis=0
    ).astype(bf16)

    def exchange(rows):
        moved = lax.all_to_all(
            rows.reshape(experts, capacity, features),
            ("expert", "dp"),
            split_axis=0,
            concat_axis=0,
            tiled=True,
        )
        return moved.reshape(rows_total, features)

    send_x = jnp.einsum("ts,td->sd", place, tokens, preferred_element_type=f32).astype(bf16)
    recv_x = exchange(send_x)
    send_dy = jnp.einsum("ts,td->sd", weigh, out_grad, preferred_element_type=f32).astype(bf16)
    recv_dy = exchange(send_dy)
    gate_full = lax.all_gather(gate_weight[0], "sub", axis=0, tiled=True)
    up_full = lax.all_gather(up_weight[0], "sub", axis=0, tiled=True)
    down_full = lax.all_gather(down_weight[0], "sub", axis=0, tiled=True)

    gate = jnp.einsum("rd,fd->rf", recv_x, gate_full, preferred_element_type=f32)
    up = jnp.einsum("rd,fd->rf", recv_x, up_full, preferred_element_type=f32)
    sigmoid = jax.nn.sigmoid(gate)
    hidden = lax.optimization_barrier((gate * sigmoid * up).astype(bf16))
    output = jnp.einsum("rf,fd->rd", hidden, down_full, preferred_element_type=f32).astype(bf16)
    output, recv_dy = lax.optimization_barrier((output, recv_dy))
    back_out = exchange(output)

    hidden_grad = jnp.einsum("rd,fd->rf", recv_dy, down_full, preferred_element_type=f32)
    gate_delta = (hidden_grad * up * sigmoid * (1.0 + gate * (1.0 - sigmoid))).astype(bf16)
    up_delta = (hidden_grad * gate * sigmoid).astype(bf16)
    input_grad = (
        jnp.einsum("rf,fd->rd", gate_delta, gate_full, preferred_element_type=f32)
        + jnp.einsum("rf,fd->rd", up_delta, up_full, preferred_element_type=f32)
    ).astype(bf16)
    back_grad = exchange(input_grad)

    def weight_grad(left, right):
        part = jnp.einsum("rf,rd->fd", left, right, preferred_element_type=f32).astype(bf16)
        return lax.psum_scatter(part, "sub", scatter_dimension=0, tiled=True)[None]

    down_grad = weight_grad(hidden, recv_dy)
    gate_grad = weight_grad(gate_delta, recv_x)
    up_grad = weight_grad(up_delta, recv_x)

    weights = route_weights.astype(f32)
    cotangent = out_grad.astype(f32)
    visit = [jnp.dot(pick[k], back_out, preferred_element_type=f32) for k in range(top_count)]
    mixed = sum(weights[:, k : k + 1] * visit[k] for k in range(top_count)).astype(bf16)
    route_grad = jnp.stack([jnp.sum(cotangent * v, axis=1) for v in visit], axis=1)
    token_grad = jnp.einsum("ts,sd->td", place, back_grad, preferred_element_type=f32).astype(bf16)
    return (mixed, token_grad, route_grad, gate_grad, up_grad, down_grad)


def solution(mesh):
    rows = P(("groups", "expert", "dp", "sub"), None)
    weight = P(("expert", "dp"), "sub", None)
    grad = P(("groups", "expert", "dp"), "sub", None)
    return jax.shard_map(
        shards,
        mesh=mesh,
        in_specs=(rows,) * 4 + (weight,) * 3,
        out_specs=(rows,) * 3 + (grad,) * 3,
        check_vma=False,
    )
```

```python
import functools

import jax
import jax.numpy as jnp
from jax import lax
from jax.experimental import pallas as pl
from jax.experimental.pallas import tpu as pltpu
from jax.sharding import PartitionSpec as P


def dot(left, right, dims=((1,), (0,))):
    return lax.dot_general(left, right, (dims, ((), ())), preferred_element_type=jnp.float32)


def fused(
    experts, replicas, capacity,
    send_x, send_dy, gate_in, up_in, down_in, pick0, pick1, place, weights, cotangent,
    mixed, token_grad, route_grad, gate_grad, up_grad, down_grad,
    recv_x, recv_dy, out_send, grad_send, back_out, back_grad,
    w_full, factor_gate, factor_up, hidden, gate_delta, up_delta, turned,
    part_send, part_recv, part_own,
    row_send, row_recv, core_send, core_recv,
):
    f32, bf16 = jnp.float32, jnp.bfloat16
    me = lax.axis_index("expert") * replicas + lax.axis_index("dp")
    core = lax.axis_index("sub")
    half = gate_in.shape[0]
    mesh_id = pl.DeviceIdType.MESH

    def device(index):
        return {"expert": lax.div(index, replicas), "dp": lax.rem(index, replicas)}

    barrier = pltpu.get_barrier_semaphore()
    for r in range(1, experts):
        pl.semaphore_signal(
            barrier, inc=1, device_id=device(lax.rem(me + r, experts)), device_id_type=mesh_id
        )
    pl.semaphore_signal(barrier, inc=1, device_id={"sub": 1 - core}, device_id_type=mesh_id)
    pl.semaphore_wait(barrier, experts)

    def block(index):
        return pl.ds(pl.multiple_of(index * capacity, 16), capacity)

    def unit_rows(index):
        return pl.ds(pl.multiple_of(index * half, 16), half)

    def exchange(which, source, landing):
        copies = []
        for r in range(1, experts):
            to = lax.rem(me + r, experts)
            copy = pltpu.make_async_remote_copy(
                src_ref=source.at[block(to)],
                dst_ref=landing.at[block(me)],
                send_sem=row_send.at[which, r],
                recv_sem=row_recv.at[which, r],
                device_id=device(to),
                device_id_type=mesh_id,
            )
            copy.start()
            copies.append(copy)
        landing[block(me), :] = source[block(me), :]
        return copies

    def to_core(slot, source, landing):
        copy = pltpu.make_async_remote_copy(
            src_ref=source,
            dst_ref=landing,
            send_sem=core_send.at[slot],
            recv_sem=core_recv.at[slot],
            device_id={"sub": 1 - core},
            device_id_type=mesh_id,
        )
        copy.start()
        return copy

    def finish(copies):
        for copy in copies:
            copy.wait()

    x_copies = exchange(0, send_x, recv_x)
    w_copies = []
    for k, ref in enumerate((gate_in, up_in, down_in)):
        w_copies.append(to_core(k, ref, w_full.at[k, unit_rows(core)]))
        w_full[k, unit_rows(core), :] = ref[...]
    dy_copies = exchange(1, send_dy, recv_dy)
    finish(w_copies)
    finish(x_copies)

    total = recv_x.shape[0]
    step = total // 2

    def forward(i, carry):
        rows = pl.ds(pl.multiple_of(i * step, 16), step)
        x = recv_x[rows, :]
        gate = dot(x, w_full[0], ((1,), (1,)))
        up = dot(x, w_full[1], ((1,), (1,)))
        sigmoid = jax.nn.sigmoid(gate)
        act = gate * sigmoid
        rounded = (act * up).astype(bf16)
        hidden[rows, :] = rounded
        factor_gate[rows, :] = up * sigmoid * (1.0 + gate * (1.0 - sigmoid))
        factor_up[rows, :] = act
        out_send[rows, :] = dot(rounded, w_full[2]).astype(bf16)
        return carry

    lax.fori_loop(0, 2, forward, 0)
    out_copies = exchange(2, out_send, back_out)
    finish(dy_copies)

    def backward(i, carry):
        rows = pl.ds(pl.multiple_of(i * step, 16), step)
        back = dot(recv_dy[rows, :], w_full[2], ((1,), (1,)))
        by_gate = (back * factor_gate[rows, :]).astype(bf16)
        by_up = (back * factor_up[rows, :]).astype(bf16)
        gate_delta[rows, :] = by_gate
        up_delta[rows, :] = by_up
        grad_send[rows, :] = (dot(by_gate, w_full[0]) + dot(by_up, w_full[1])).astype(bf16)
        return carry

    lax.fori_loop(0, 2, backward, 0)
    grad_copies = exchange(3, grad_send, back_grad)

    part_copies = []
    sides = ((hidden, recv_dy), (gate_delta, recv_x), (up_delta, recv_x))
    for k, (left, right) in enumerate(sides):
        turned[...] = left[...].astype(f32).T.astype(bf16)
        part_send[k] = dot(turned[unit_rows(1 - core), :], right[...]).astype(bf16)
        part_copies.append(to_core(3 + k, part_send.at[k], part_recv.at[k]))
        part_own[k] = dot(turned[unit_rows(core), :], right[...]).astype(bf16)
    finish(part_copies)
    for k, ref in enumerate((down_grad, gate_grad, up_grad)):
        ref[...] = (part_own[k].astype(f32) + part_recv[k].astype(f32)).astype(bf16)

    finish(out_copies)
    dy = cotangent[...].astype(f32)
    first = dot(pick0[...], back_out[...])
    second = dot(pick1[...], back_out[...])
    mixed[...] = (weights[:, 0:1] * first + weights[:, 1:2] * second).astype(bf16)
    route_grad[:, 0:1] = jnp.sum(dy * first, axis=1, keepdims=True)
    route_grad[:, 1:2] = jnp.sum(dy * second, axis=1, keepdims=True)
    finish(grad_copies)
    token_grad[...] = dot(place[...], back_grad[...]).astype(bf16)


def shards(tokens, expert_ids, route_weights, out_grad, gate_weight, up_weight, down_weight):
    f32, bf16 = jnp.float32, jnp.bfloat16
    tok_rows, features = tokens.shape
    top_count = expert_ids.shape[1]
    experts = lax.axis_size("expert") * lax.axis_size("dp")
    capacity = max(2, 3 * tok_rows * top_count // (2 * experts))
    rows_total = experts * capacity

    hit = expert_ids[:, :, None] == jnp.arange(experts, dtype=jnp.int32)[None, None, :]
    named = jnp.any(hit, axis=1).astype(bf16)
    row = jnp.arange(tok_rows)
    earlier = (row[:, None] > row[None, :]).astype(bf16)
    before = jnp.dot(earlier, named, preferred_element_type=f32)
    slot_index = jnp.sum(jnp.where(hit, before[:, None, :], 0.0), axis=2).astype(jnp.int32)
    target = expert_ids * capacity + slot_index
    slots = jnp.arange(rows_total, dtype=jnp.int32)
    picks = target.T[:, :, None] == slots[None, None, :]
    pick = picks.astype(bf16)
    place = jnp.any(picks, axis=0).astype(bf16)
    weigh = jnp.sum(
        jnp.where(picks, route_weights.T.astype(f32)[:, :, None], 0.0), axis=0
    ).astype(bf16)

    def exchange(rows):
        moved = lax.all_to_all(
            rows.reshape(experts, capacity, features),
            ("expert", "dp"),
            split_axis=0,
            concat_axis=0,
            tiled=True,
        )
        return moved.reshape(rows_total, features)

    send_x = jnp.einsum("ts,td->sd", place, tokens, preferred_element_type=f32).astype(bf16)
    send_dy = jnp.einsum("ts,td->sd", weigh, out_grad, preferred_element_type=f32).astype(bf16)
    if capacity % 16 == 0 and experts <= 8 and lax.axis_size("sub") == 2 and top_count == 2:
        units = 2 * gate_weight.shape[1]
        half = gate_weight.shape[1]
        vmem = pl.BlockSpec(memory_space=pltpu.VMEM)
        slab = pltpu.VMEM((rows_total, features), bf16)
        wide = pltpu.VMEM((rows_total, units), f32)
        slim = pltpu.VMEM((rows_total, units), bf16)
        part = pltpu.VMEM((3, half, features), bf16)
        like = jax.ShapeDtypeStruct
        results = pl.pallas_call(
            functools.partial(fused, experts, lax.axis_size("dp"), capacity),
            out_shape=(
                like((tok_rows, features), bf16),
                like((tok_rows, features), bf16),
                like((tok_rows, top_count), f32),
            )
            + (like((half, features), bf16),) * 3,
            in_specs=[vmem] * 10,
            out_specs=(vmem,) * 6,
            scratch_shapes=[slab] * 6
            + [pltpu.VMEM((3, units, features), bf16), wide, wide, slim, slim, slim]
            + [pltpu.VMEM((units, rows_total), bf16), part, part, part]
            + [pltpu.SemaphoreType.DMA((4, experts))] * 2
            + [pltpu.SemaphoreType.DMA((6,))] * 2,
            compiler_params=pltpu.CompilerParams(
                collective_id=0, has_side_effects=True, vmem_limit_bytes=48 * 1024 * 1024
            ),
        )(
            send_x, send_dy, gate_weight[0], up_weight[0], down_weight[0],
            pick[0], pick[1], place, route_weights.astype(f32), out_grad,
        )
        return results[:3] + tuple(r[None] for r in results[3:])
    recv_x = exchange(send_x)
    recv_dy = exchange(send_dy)
    gate_full = lax.all_gather(gate_weight[0], "sub", axis=0, tiled=True)
    up_full = lax.all_gather(up_weight[0], "sub", axis=0, tiled=True)
    down_full = lax.all_gather(down_weight[0], "sub", axis=0, tiled=True)

    gate = jnp.einsum("rd,fd->rf", recv_x, gate_full, preferred_element_type=f32)
    up = jnp.einsum("rd,fd->rf", recv_x, up_full, preferred_element_type=f32)
    sigmoid = jax.nn.sigmoid(gate)
    hidden = lax.optimization_barrier((gate * sigmoid * up).astype(bf16))
    output = jnp.einsum("rf,fd->rd", hidden, down_full, preferred_element_type=f32).astype(bf16)
    output, recv_dy = lax.optimization_barrier((output, recv_dy))
    back_out = exchange(output)

    hidden_grad = jnp.einsum("rd,fd->rf", recv_dy, down_full, preferred_element_type=f32)
    gate_delta = (hidden_grad * up * sigmoid * (1.0 + gate * (1.0 - sigmoid))).astype(bf16)
    up_delta = (hidden_grad * gate * sigmoid).astype(bf16)
    input_grad = (
        jnp.einsum("rf,fd->rd", gate_delta, gate_full, preferred_element_type=f32)
        + jnp.einsum("rf,fd->rd", up_delta, up_full, preferred_element_type=f32)
    ).astype(bf16)
    back_grad = exchange(input_grad)

    def weight_grad(left, right):
        part = jnp.einsum("rf,rd->fd", left, right, preferred_element_type=f32).astype(bf16)
        return lax.psum_scatter(part, "sub", scatter_dimension=0, tiled=True)[None]

    down_grad = weight_grad(hidden, recv_dy)
    gate_grad = weight_grad(gate_delta, recv_x)
    up_grad = weight_grad(up_delta, recv_x)

    weights = route_weights.astype(f32)
    cotangent = out_grad.astype(f32)
    visit = [jnp.dot(pick[k], back_out, preferred_element_type=f32) for k in range(top_count)]
    mixed = sum(weights[:, k : k + 1] * visit[k] for k in range(top_count)).astype(bf16)
    route_grad = jnp.stack([jnp.sum(cotangent * v, axis=1) for v in visit], axis=1)
    token_grad = jnp.einsum("ts,sd->td", place, back_grad, preferred_element_type=f32).astype(bf16)
    return (mixed, token_grad, route_grad, gate_grad, up_grad, down_grad)


def solution(mesh):
    rows = P(("groups", "expert", "dp", "sub"), None)
    weight = P(("expert", "dp"), "sub", None)
    grad = P(("groups", "expert", "dp"), "sub", None)
    return jax.shard_map(
        shards,
        mesh=mesh,
        in_specs=(rows,) * 4 + (weight,) * 3,
        out_specs=(rows,) * 3 + (grad,) * 3,
        check_vma=False,
    )
```

```python
import functools

import jax
import jax.numpy as jnp
from jax import lax
from jax.experimental import pallas as pl
from jax.experimental.pallas import tpu as pltpu
from jax.sharding import PartitionSpec as P


def dot(left, right, dims=((1,), (0,))):
    return lax.dot_general(left, right, (dims, ((), ())), preferred_element_type=jnp.float32)


def fused(
    experts, replicas, capacity,
    tokens, cotangent, gate_in, up_in, down_in, target, target_t, weights, weights_t,
    mixed, token_grad, route_grad, gate_grad, up_grad, down_grad,
    place_t, weigh_t, send_x, send_dy, recv_x, recv_dy, out_send, grad_send, back_out, back_grad,
    w_full, factor_gate, factor_up, hidden, gate_delta, up_delta, turned,
    part_send, part_recv, part_own,
    row_send, row_recv, core_send, core_recv,
):
    f32, bf16 = jnp.float32, jnp.bfloat16
    me = lax.axis_index("expert") * replicas + lax.axis_index("dp")
    core = lax.axis_index("sub")
    half = gate_in.shape[0]
    mesh_id = pl.DeviceIdType.MESH

    def device(index):
        return {"expert": lax.div(index, replicas), "dp": lax.rem(index, replicas)}

    barrier = pltpu.get_barrier_semaphore()
    def peer(r):
        index, bit = 0, 1
        while bit < experts:
            own = lax.rem(lax.div(me, bit), 2)
            index = index + bit * (1 - own if r & bit else own)
            bit *= 2
        return index

    for r in range(1, experts):
        pl.semaphore_signal(barrier, inc=1, device_id=device(peer(r)), device_id_type=mesh_id)
    pl.semaphore_signal(barrier, inc=1, device_id={"sub": 1 - core}, device_id_type=mesh_id)

    slot = lax.broadcasted_iota(jnp.int32, place_t.shape, 0)
    at_first, at_second = slot == target_t[0:1, :], slot == target_t[1:2, :]
    place_t[...] = jnp.where(at_first | at_second, 1.0, 0.0).astype(bf16)
    weigh_t[...] = jnp.where(
        at_first, weights_t[0:1, :], jnp.where(at_second, weights_t[1:2, :], 0.0)
    ).astype(bf16)
    pl.semaphore_wait(barrier, experts)

    def block(index):
        return pl.ds(pl.multiple_of(index * capacity, 16), capacity)

    def unit_rows(index):
        return pl.ds(pl.multiple_of(index * half, 16), half)

    def exchange(which, source, landing, fill=None):
        copies = []
        for r in range(experts - 1, 0, -1):
            to = peer(r)
            if fill is not None:
                fill(to)
            copy = pltpu.make_async_remote_copy(
                src_ref=source.at[block(to)],
                dst_ref=landing.at[block(me)],
                send_sem=row_send.at[which, r],
                recv_sem=row_recv.at[which, r],
                device_id=device(to),
                device_id_type=mesh_id,
            )
            copy.start()
            copies.append(copy)
        if fill is not None:
            fill(me)
        landing[block(me), :] = source[block(me), :]
        return copies

    def to_core(slot, source, landing):
        copy = pltpu.make_async_remote_copy(
            src_ref=source,
            dst_ref=landing,
            send_sem=core_send.at[slot],
            recv_sem=core_recv.at[slot],
            device_id={"sub": 1 - core},
            device_id_type=mesh_id,
        )
        copy.start()
        return copy

    def finish(copies):
        for copy in copies:
            copy.wait()

    def fill_x(e):
        send_x[block(e), :] = dot(place_t[block(e), :], tokens[...]).astype(bf16)

    def fill_dy(e):
        send_dy[block(e), :] = dot(weigh_t[block(e), :], cotangent[...]).astype(bf16)

    x_copies = exchange(0, send_x, recv_x, fill_x)
    w_copies = []
    for k, ref in enumerate((gate_in, up_in, down_in)):
        w_copies.append(to_core(k, ref, w_full.at[k, unit_rows(core)]))
        w_full[k, unit_rows(core), :] = ref[...]
    dy_copies = exchange(1, send_dy, recv_dy, fill_dy)
    finish(w_copies)
    finish(x_copies)

    total = recv_x.shape[0]
    step = total // 2

    def forward(i, carry):
        rows = pl.ds(pl.multiple_of(i * step, 16), step)
        x = recv_x[rows, :]
        gate = dot(x, w_full[0], ((1,), (1,)))
        up = dot(x, w_full[1], ((1,), (1,)))
        sigmoid = jax.nn.sigmoid(gate)
        act = gate * sigmoid
        rounded = (act * up).astype(bf16)
        hidden[rows, :] = rounded
        factor_gate[rows, :] = up * sigmoid * (1.0 + gate * (1.0 - sigmoid))
        factor_up[rows, :] = act
        out_send[rows, :] = dot(rounded, w_full[2]).astype(bf16)
        return carry

    lax.fori_loop(0, 2, forward, 0)
    out_copies = exchange(2, out_send, back_out)
    finish(dy_copies)

    def backward(i, carry):
        rows = pl.ds(pl.multiple_of(i * step, 16), step)
        back = dot(recv_dy[rows, :], w_full[2], ((1,), (1,)))
        by_gate = (back * factor_gate[rows, :]).astype(bf16)
        by_up = (back * factor_up[rows, :]).astype(bf16)
        gate_delta[rows, :] = by_gate
        up_delta[rows, :] = by_up
        grad_send[rows, :] = (dot(by_gate, w_full[0]) + dot(by_up, w_full[1])).astype(bf16)
        return carry

    lax.fori_loop(0, 2, backward, 0)
    grad_copies = exchange(3, grad_send, back_grad)

    part_copies = []
    sides = ((hidden, recv_dy), (gate_delta, recv_x), (up_delta, recv_x))
    for k, (left, right) in enumerate(sides):
        turned[...] = left[...].astype(f32).T.astype(bf16)
        part_send[k] = dot(turned[unit_rows(1 - core), :], right[...]).astype(bf16)
        part_copies.append(to_core(3 + k, part_send.at[k], part_recv.at[k]))
        part_own[k] = dot(turned[unit_rows(core), :], right[...]).astype(bf16)
    finish(part_copies)
    for k, ref in enumerate((down_grad, gate_grad, up_grad)):
        ref[...] = (part_own[k].astype(f32) + part_recv[k].astype(f32)).astype(bf16)

    finish(out_copies)
    dy = cotangent[...].astype(f32)
    lane = lax.broadcasted_iota(jnp.int32, (target.shape[0], total), 1)
    pick0 = jnp.where(lane == target[:, 0:1], 1.0, 0.0)
    pick1 = jnp.where(lane == target[:, 1:2], 1.0, 0.0)
    first = dot(pick0.astype(bf16), back_out[...])
    second = dot(pick1.astype(bf16), back_out[...])
    mixed[...] = (weights[:, 0:1] * first + weights[:, 1:2] * second).astype(bf16)
    route_grad[:, 0:1] = jnp.sum(dy * first, axis=1, keepdims=True)
    route_grad[:, 1:2] = jnp.sum(dy * second, axis=1, keepdims=True)
    finish(grad_copies)
    token_grad[...] = dot((pick0 + pick1).astype(bf16), back_grad[...]).astype(bf16)


def shards(tokens, expert_ids, route_weights, out_grad, gate_weight, up_weight, down_weight):
    f32, bf16 = jnp.float32, jnp.bfloat16
    tok_rows, features = tokens.shape
    top_count = expert_ids.shape[1]
    experts = lax.axis_size("expert") * lax.axis_size("dp")
    capacity = max(2, 3 * tok_rows * top_count // (2 * experts))
    rows_total = experts * capacity

    hit = expert_ids[:, :, None] == jnp.arange(experts, dtype=jnp.int32)[None, None, :]
    named = jnp.any(hit, axis=1).astype(bf16)
    row = jnp.arange(tok_rows)
    earlier = (row[:, None] > row[None, :]).astype(bf16)
    before = jnp.dot(earlier, named, preferred_element_type=f32)
    slot_index = jnp.sum(jnp.where(hit, before[:, None, :], 0.0), axis=2).astype(jnp.int32)
    target = expert_ids * capacity + slot_index
    if capacity % 16 == 0 and experts in (2, 4, 8) and lax.axis_size("sub") == 2 and top_count == 2:
        units = 2 * gate_weight.shape[1]
        half = gate_weight.shape[1]
        vmem = pl.BlockSpec(memory_space=pltpu.VMEM)
        slab = pltpu.VMEM((rows_total, features), bf16)
        wide = pltpu.VMEM((rows_total, units), f32)
        slim = pltpu.VMEM((rows_total, units), bf16)
        part = pltpu.VMEM((3, half, features), bf16)
        like = jax.ShapeDtypeStruct
        results = pl.pallas_call(
            functools.partial(fused, experts, lax.axis_size("dp"), capacity),
            out_shape=(
                like((tok_rows, features), bf16),
                like((tok_rows, features), bf16),
                like((tok_rows, top_count), f32),
            )
            + (like((half, features), bf16),) * 3,
            in_specs=[vmem] * 9,
            out_specs=(vmem,) * 6,
            scratch_shapes=[pltpu.VMEM((rows_total, tok_rows), bf16)] * 2 + [slab] * 8
            + [pltpu.VMEM((3, units, features), bf16), wide, wide, slim, slim, slim]
            + [pltpu.VMEM((units, rows_total), bf16), part, part, part]
            + [pltpu.SemaphoreType.DMA((4, experts))] * 2
            + [pltpu.SemaphoreType.DMA((6,))] * 2,
            compiler_params=pltpu.CompilerParams(
                collective_id=0, has_side_effects=True, vmem_limit_bytes=48 * 1024 * 1024
            ),
        )(
            tokens, out_grad, gate_weight[0], up_weight[0], down_weight[0],
            target, target.T, route_weights.astype(f32), route_weights.T.astype(f32),
        )
        return results[:3] + tuple(r[None] for r in results[3:])

    slots = jnp.arange(rows_total, dtype=jnp.int32)
    picks = target.T[:, :, None] == slots[None, None, :]
    pick = picks.astype(bf16)
    place = jnp.any(picks, axis=0).astype(bf16)
    weigh = jnp.sum(
        jnp.where(picks, route_weights.T.astype(f32)[:, :, None], 0.0), axis=0
    ).astype(bf16)

    def exchange(rows):
        moved = lax.all_to_all(
            rows.reshape(experts, capacity, features),
            ("expert", "dp"),
            split_axis=0,
            concat_axis=0,
            tiled=True,
        )
        return moved.reshape(rows_total, features)

    send_x = jnp.einsum("ts,td->sd", place, tokens, preferred_element_type=f32).astype(bf16)
    send_dy = jnp.einsum("ts,td->sd", weigh, out_grad, preferred_element_type=f32).astype(bf16)
    recv_x = exchange(send_x)
    recv_dy = exchange(send_dy)
    gate_full = lax.all_gather(gate_weight[0], "sub", axis=0, tiled=True)
    up_full = lax.all_gather(up_weight[0], "sub", axis=0, tiled=True)
    down_full = lax.all_gather(down_weight[0], "sub", axis=0, tiled=True)

    gate = jnp.einsum("rd,fd->rf", recv_x, gate_full, preferred_element_type=f32)
    up = jnp.einsum("rd,fd->rf", recv_x, up_full, preferred_element_type=f32)
    sigmoid = jax.nn.sigmoid(gate)
    hidden = lax.optimization_barrier((gate * sigmoid * up).astype(bf16))
    output = jnp.einsum("rf,fd->rd", hidden, down_full, preferred_element_type=f32).astype(bf16)
    output, recv_dy = lax.optimization_barrier((output, recv_dy))
    back_out = exchange(output)

    hidden_grad = jnp.einsum("rd,fd->rf", recv_dy, down_full, preferred_element_type=f32)
    gate_delta = (hidden_grad * up * sigmoid * (1.0 + gate * (1.0 - sigmoid))).astype(bf16)
    up_delta = (hidden_grad * gate * sigmoid).astype(bf16)
    input_grad = (
        jnp.einsum("rf,fd->rd", gate_delta, gate_full, preferred_element_type=f32)
        + jnp.einsum("rf,fd->rd", up_delta, up_full, preferred_element_type=f32)
    ).astype(bf16)
    back_grad = exchange(input_grad)

    def weight_grad(left, right):
        part = jnp.einsum("rf,rd->fd", left, right, preferred_element_type=f32).astype(bf16)
        return lax.psum_scatter(part, "sub", scatter_dimension=0, tiled=True)[None]

    down_grad = weight_grad(hidden, recv_dy)
    gate_grad = weight_grad(gate_delta, recv_x)
    up_grad = weight_grad(up_delta, recv_x)

    weights = route_weights.astype(f32)
    cotangent = out_grad.astype(f32)
    visit = [jnp.dot(pick[k], back_out, preferred_element_type=f32) for k in range(top_count)]
    mixed = sum(weights[:, k : k + 1] * visit[k] for k in range(top_count)).astype(bf16)
    route_grad = jnp.stack([jnp.sum(cotangent * v, axis=1) for v in visit], axis=1)
    token_grad = jnp.einsum("ts,sd->td", place, back_grad, preferred_element_type=f32).astype(bf16)
    return (mixed, token_grad, route_grad, gate_grad, up_grad, down_grad)


def solution(mesh):
    rows = P(("groups", "expert", "dp", "sub"), None)
    weight = P(("expert", "dp"), "sub", None)
    grad = P(("groups", "expert", "dp"), "sub", None)
    return jax.shard_map(
        shards,
        mesh=mesh,
        in_specs=(rows,) * 4 + (weight,) * 3,
        out_specs=(rows,) * 3 + (grad,) * 3,
        check_vma=False,
    )
```

```python
import functools

import jax
import jax.numpy as jnp
from jax import lax
from jax.experimental import pallas as pl
from jax.experimental.pallas import tpu as pltpu
from jax.sharding import PartitionSpec as P


def dot(left, right, dims=((1,), (0,))):
    return lax.dot_general(left, right, (dims, ((), ())), preferred_element_type=jnp.float32)


def fused(
    experts, replicas, capacity,
    tokens_in, cotangent_in, gate_in, up_in, down_in, target, target_t, weights, weights_t,
    mixed, token_grad, route_grad, gate_grad, up_grad, down_grad,
    place_t, weigh_t, send_x, send_dy, recv_x, recv_dy, out_send, grad_send, back_out, back_grad,
    w_full, factor_gate, factor_up, hidden, gate_delta, up_delta, turned,
    part_send, part_recv, part_own,
    row_send, row_recv, core_send, core_recv, tokens, cotangent, loaded,
):
    f32, bf16 = jnp.float32, jnp.bfloat16
    me = lax.axis_index("expert") * replicas + lax.axis_index("dp")
    core = lax.axis_index("sub")
    half = gate_in.shape[0]
    mesh_id = pl.DeviceIdType.MESH

    def device(index):
        return {"expert": lax.div(index, replicas), "dp": lax.rem(index, replicas)}

    barrier = pltpu.get_barrier_semaphore()
    def peer(r):
        return lax.rem(me + r, experts)

    loads = []
    sources = (tokens_in, cotangent_in, gate_in, up_in, down_in)
    own_rows = pl.ds(pl.multiple_of(core * half, 16), half)
    landings = (tokens, cotangent) + tuple(w_full.at[k, own_rows] for k in range(3))
    for k in range(5):
        load = pltpu.make_async_copy(sources[k], landings[k], loaded.at[k])
        load.start()
        loads.append(load)

    for r in range(1, experts):
        pl.semaphore_signal(barrier, inc=1, device_id=device(peer(r)), device_id_type=mesh_id)
    pl.semaphore_signal(barrier, inc=1, device_id={"sub": 1 - core}, device_id_type=mesh_id)

    slot = lax.broadcasted_iota(jnp.int32, place_t.shape, 0)
    at_first, at_second = slot == target_t[0:1, :], slot == target_t[1:2, :]
    place_t[...] = jnp.where(at_first | at_second, 1.0, 0.0).astype(bf16)
    weigh_t[...] = jnp.where(
        at_first, weights_t[0:1, :], jnp.where(at_second, weights_t[1:2, :], 0.0)
    ).astype(bf16)
    pl.semaphore_wait(barrier, experts)

    def block(index):
        return pl.ds(pl.multiple_of(index * capacity, 16), capacity)

    def unit_rows(index):
        return pl.ds(pl.multiple_of(index * half, 16), half)

    def exchange(which, source, landing, fill=None):
        copies = []
        for r in range(1, experts):
            to = peer(r)
            if fill is not None:
                fill(to)
            copy = pltpu.make_async_remote_copy(
                src_ref=source.at[block(to)],
                dst_ref=landing.at[block(me)],
                send_sem=row_send.at[which, r],
                recv_sem=row_recv.at[which, r],
                device_id=device(to),
                device_id_type=mesh_id,
            )
            copy.start()
            copies.append(copy)
        if fill is not None:
            fill(me)
        landing[block(me), :] = source[block(me), :]
        return copies

    def to_core(slot, source, landing):
        copy = pltpu.make_async_remote_copy(
            src_ref=source,
            dst_ref=landing,
            send_sem=core_send.at[slot],
            recv_sem=core_recv.at[slot],
            device_id={"sub": 1 - core},
            device_id_type=mesh_id,
        )
        copy.start()
        return copy

    def finish(copies):
        for copy in copies:
            copy.wait()

    def fill_x(e):
        send_x[block(e), :] = dot(place_t[block(e), :], tokens[...]).astype(bf16)

    def fill_dy(e):
        send_dy[block(e), :] = dot(weigh_t[block(e), :], cotangent[...]).astype(bf16)

    loads[0].wait()
    x_copies = exchange(0, send_x, recv_x, fill_x)
    w_copies = []
    for k, ref in enumerate((gate_in, up_in, down_in)):
        w_copies.append(to_core(k, ref, w_full.at[k, unit_rows(core)]))
    loads[1].wait()
    dy_copies = exchange(1, send_dy, recv_dy, fill_dy)
    finish(w_copies)
    finish(loads[2:])
    finish(x_copies)

    total = recv_x.shape[0]
    step = total // 2

    def forward(i, carry):
        rows = pl.ds(pl.multiple_of(i * step, 16), step)
        x = recv_x[rows, :]
        gate = dot(x, w_full[0], ((1,), (1,)))
        up = dot(x, w_full[1], ((1,), (1,)))
        sigmoid = jax.nn.sigmoid(gate)
        act = gate * sigmoid
        rounded = (act * up).astype(bf16)
        hidden[rows, :] = rounded
        factor_gate[rows, :] = up * sigmoid * (1.0 + gate * (1.0 - sigmoid))
        factor_up[rows, :] = act
        out_send[rows, :] = dot(rounded, w_full[2]).astype(bf16)
        return carry

    lax.fori_loop(0, 2, forward, 0)
    out_copies = exchange(2, out_send, back_out)
    finish(dy_copies)

    def backward(i, carry):
        rows = pl.ds(pl.multiple_of(i * step, 16), step)
        back = dot(recv_dy[rows, :], w_full[2], ((1,), (1,)))
        by_gate = (back * factor_gate[rows, :]).astype(bf16)
        by_up = (back * factor_up[rows, :]).astype(bf16)
        gate_delta[rows, :] = by_gate
        up_delta[rows, :] = by_up
        grad_send[rows, :] = (dot(by_gate, w_full[0]) + dot(by_up, w_full[1])).astype(bf16)
        return carry

    lax.fori_loop(0, 2, backward, 0)
    grad_copies = exchange(3, grad_send, back_grad)

    part_copies = []
    sides = ((hidden, recv_dy), (gate_delta, recv_x), (up_delta, recv_x))
    for k, (left, right) in enumerate(sides):
        turned[...] = left[...].astype(f32).T.astype(bf16)
        part_send[k] = dot(turned[unit_rows(1 - core), :], right[...]).astype(bf16)
        part_copies.append(to_core(3 + k, part_send.at[k], part_recv.at[k]))
        part_own[k] = dot(turned[unit_rows(core), :], right[...]).astype(bf16)
    finish(part_copies)
    for k, ref in enumerate((down_grad, gate_grad, up_grad)):
        ref[...] = (part_own[k].astype(f32) + part_recv[k].astype(f32)).astype(bf16)

    finish(out_copies)
    dy = cotangent[...].astype(f32)
    lane = lax.broadcasted_iota(jnp.int32, (target.shape[0], total), 1)
    pick0 = jnp.where(lane == target[:, 0:1], 1.0, 0.0)
    pick1 = jnp.where(lane == target[:, 1:2], 1.0, 0.0)
    first = dot(pick0.astype(bf16), back_out[...])
    second = dot(pick1.astype(bf16), back_out[...])
    mixed[...] = (weights[:, 0:1] * first + weights[:, 1:2] * second).astype(bf16)
    route_grad[:, 0:1] = jnp.sum(dy * first, axis=1, keepdims=True)
    route_grad[:, 1:2] = jnp.sum(dy * second, axis=1, keepdims=True)
    finish(grad_copies)
    token_grad[...] = dot((pick0 + pick1).astype(bf16), back_grad[...]).astype(bf16)


def shards(tokens, expert_ids, route_weights, out_grad, gate_weight, up_weight, down_weight):
    f32, bf16 = jnp.float32, jnp.bfloat16
    tok_rows, features = tokens.shape
    top_count = expert_ids.shape[1]
    experts = lax.axis_size("expert") * lax.axis_size("dp")
    capacity = max(2, 3 * tok_rows * top_count // (2 * experts))
    rows_total = experts * capacity

    hit = expert_ids[:, :, None] == jnp.arange(experts, dtype=jnp.int32)[None, None, :]
    named = jnp.any(hit, axis=1).astype(bf16)
    row = jnp.arange(tok_rows)
    earlier = (row[:, None] > row[None, :]).astype(bf16)
    before = jnp.dot(earlier, named, preferred_element_type=f32)
    slot_index = jnp.sum(jnp.where(hit, before[:, None, :], 0.0), axis=2).astype(jnp.int32)
    target = expert_ids * capacity + slot_index
    if capacity % 16 == 0 and experts in (2, 4, 8) and lax.axis_size("sub") == 2 and top_count == 2:
        units = 2 * gate_weight.shape[1]
        half = gate_weight.shape[1]
        vmem = pl.BlockSpec(memory_space=pltpu.VMEM)
        slab = pltpu.VMEM((rows_total, features), bf16)
        wide = pltpu.VMEM((rows_total, units), f32)
        slim = pltpu.VMEM((rows_total, units), bf16)
        part = pltpu.VMEM((3, half, features), bf16)
        like = jax.ShapeDtypeStruct
        results = pl.pallas_call(
            functools.partial(fused, experts, lax.axis_size("dp"), capacity),
            out_shape=(
                like((tok_rows, features), bf16),
                like((tok_rows, features), bf16),
                like((tok_rows, top_count), f32),
            )
            + (like((half, features), bf16),) * 3,
            in_specs=[pl.BlockSpec(memory_space=pltpu.HBM)] * 5 + [vmem] * 4,
            out_specs=(vmem,) * 6,
            scratch_shapes=[pltpu.VMEM((rows_total, tok_rows), bf16)] * 2 + [slab] * 8
            + [pltpu.VMEM((3, units, features), bf16), wide, wide, slim, slim, slim]
            + [pltpu.VMEM((units, rows_total), bf16), part, part, part]
            + [pltpu.SemaphoreType.DMA((4, experts))] * 2
            + [pltpu.SemaphoreType.DMA((6,))] * 2
            + [pltpu.VMEM((tok_rows, features), bf16)] * 2
            + [pltpu.SemaphoreType.DMA((5,))],
            compiler_params=pltpu.CompilerParams(
                collective_id=0, has_side_effects=True, vmem_limit_bytes=60 * 1024 * 1024
            ),
        )(
            tokens, out_grad, gate_weight[0], up_weight[0], down_weight[0],
            target, target.T, route_weights.astype(f32), route_weights.T.astype(f32),
        )
        return results[:3] + tuple(r[None] for r in results[3:])

    slots = jnp.arange(rows_total, dtype=jnp.int32)
    picks = target.T[:, :, None] == slots[None, None, :]
    pick = picks.astype(bf16)
    place = jnp.any(picks, axis=0).astype(bf16)
    weigh = jnp.sum(
        jnp.where(picks, route_weights.T.astype(f32)[:, :, None], 0.0), axis=0
    ).astype(bf16)

    def exchange(rows):
        moved = lax.all_to_all(
            rows.reshape(experts, capacity, features),
            ("expert", "dp"),
            split_axis=0,
            concat_axis=0,
            tiled=True,
        )
        return moved.reshape(rows_total, features)

    send_x = jnp.einsum("ts,td->sd", place, tokens, preferred_element_type=f32).astype(bf16)
    send_dy = jnp.einsum("ts,td->sd", weigh, out_grad, preferred_element_type=f32).astype(bf16)
    recv_x = exchange(send_x)
    recv_dy = exchange(send_dy)
    gate_full = lax.all_gather(gate_weight[0], "sub", axis=0, tiled=True)
    up_full = lax.all_gather(up_weight[0], "sub", axis=0, tiled=True)
    down_full = lax.all_gather(down_weight[0], "sub", axis=0, tiled=True)

    gate = jnp.einsum("rd,fd->rf", recv_x, gate_full, preferred_element_type=f32)
    up = jnp.einsum("rd,fd->rf", recv_x, up_full, preferred_element_type=f32)
    sigmoid = jax.nn.sigmoid(gate)
    hidden = lax.optimization_barrier((gate * sigmoid * up).astype(bf16))
    output = jnp.einsum("rf,fd->rd", hidden, down_full, preferred_element_type=f32).astype(bf16)
    output, recv_dy = lax.optimization_barrier((output, recv_dy))
    back_out = exchange(output)

    hidden_grad = jnp.einsum("rd,fd->rf", recv_dy, down_full, preferred_element_type=f32)
    gate_delta = (hidden_grad * up * sigmoid * (1.0 + gate * (1.0 - sigmoid))).astype(bf16)
    up_delta = (hidden_grad * gate * sigmoid).astype(bf16)
    input_grad = (
        jnp.einsum("rf,fd->rd", gate_delta, gate_full, preferred_element_type=f32)
        + jnp.einsum("rf,fd->rd", up_delta, up_full, preferred_element_type=f32)
    ).astype(bf16)
    back_grad = exchange(input_grad)

    def weight_grad(left, right):
        part = jnp.einsum("rf,rd->fd", left, right, preferred_element_type=f32).astype(bf16)
        return lax.psum_scatter(part, "sub", scatter_dimension=0, tiled=True)[None]

    down_grad = weight_grad(hidden, recv_dy)
    gate_grad = weight_grad(gate_delta, recv_x)
    up_grad = weight_grad(up_delta, recv_x)

    weights = route_weights.astype(f32)
    cotangent = out_grad.astype(f32)
    visit = [jnp.dot(pick[k], back_out, preferred_element_type=f32) for k in range(top_count)]
    mixed = sum(weights[:, k : k + 1] * visit[k] for k in range(top_count)).astype(bf16)
    route_grad = jnp.stack([jnp.sum(cotangent * v, axis=1) for v in visit], axis=1)
    token_grad = jnp.einsum("ts,sd->td", place, back_grad, preferred_element_type=f32).astype(bf16)
    return (mixed, token_grad, route_grad, gate_grad, up_grad, down_grad)


def solution(mesh):
    rows = P(("groups", "expert", "dp", "sub"), None)
    weight = P(("expert", "dp"), "sub", None)
    grad = P(("groups", "expert", "dp"), "sub", None)
    return jax.shard_map(
        shards,
        mesh=mesh,
        in_specs=(rows,) * 4 + (weight,) * 3,
        out_specs=(rows,) * 3 + (grad,) * 3,
        check_vma=False,
    )
```
